32 devices in a mesh: dp: 8 (over z, x), node: 4 (over y, core).
Axes of the slice: x: 2, y: 2, z: 4, core: 2. Of those that a mesh axis runs over, the one named last changes fastest.
Arguments:
- inputs: bfloat16 [4352, 12288], P(('dp', 'node')), may hold values from -6 to 6
- norm_gain: bfloat16 [12288], replicated, may hold values from 0.5 to 1.5
- cotangent: bfloat16 [4352, 128], P(('dp', 'node')), may hold values from -6 to 6
- weights: bfloat16 [12288, 128], P('dp', 'node'), may hold values from -6 to 6
- first_moment: bfloat16 [12288, 128], P('dp', 'node'), may hold values from -18 to 18
- second_moment: bfloat16 [12288, 128], P('dp', 'node'), may hold values from 1 to 30
Outputs:
- projected: bfloat16 [4352, 128], P(('dp', 'node'))
- gain_grad: float32 [12288], replicated
- new_weights: bfloat16 [12288, 128], P('dp', 'node')
- new_first: bfloat16 [12288, 128], P('dp', 'node')
- new_second: bfloat16 [12288, 128], P('dp', 'node')
The draws below stay inside these ranges and needn't reach their ends.
All inputs are finite; a program needn't handle non-finite values.
Results may differ from the reference program's by a relative error of at most 0.0024.
The reference program's roundings to bfloat16 on the way (of `normed` and `term`) count: a program that leaves them out, or rounds other values in their place, can miss the bound.
Values may be sent and summed in bfloat16 or wider, within the bound.
A program may use at most 64 MiB of HBM per device.

```python
import math
import jax
import jax.numpy as jnp
from jax import lax

D = 12288
FB = 128
TOK_DEV = 136
STEP = 20
TOKENS = 4352
DEVICES = 32


def strengthened(array, key, source, target, blocks, factor):
    owner, partner = [(jnp.arange(array.shape[position]) // (array.shape[position] // blocks)).reshape([-1 if axis == position else 1 for axis in range(array.ndim)]) for position in (source, target)]
    chosen = jax.random.permutation(key, blocks)[partner]
    strong = (owner == chosen) | (owner == (partner + blocks // 2) % blocks)
    return jnp.where(strong, factor * array, array)


def steps_of(key, dims, cuts, least, high):
    def one(position, parts):
        steps = jax.random.uniform(jax.random.fold_in(jax.random.fold_in(key, 6), position), (parts,), jnp.float32, least / len(cuts), high / len(cuts))
        return jnp.repeat(jnp.exp(steps), dims[position] // parts).reshape((-1,) + (1,) * (len(dims) - position - 1))

    factor_of = one(*cuts[0])
    for cut in cuts[1:]:
        factor_of = factor_of * one(*cut)
    return factor_of


def normal_values(own_key, dims, scale, limit, split=(), kind=jnp.bfloat16):
    array = jax.random.normal(own_key, dims, jnp.float32) * scale
    if len(split) > 0:
        array = steps_of(own_key, dims, split, -0.22, 0.18) * array
    return jnp.clip(array, min=-limit, max=limit).astype(kind)


def bell_draw_with(stream_key, extent, spread, limit, cuts, heavy, kind=jnp.bfloat16):
    drawn = spread * jax.random.normal(stream_key, extent, jnp.float32)
    if cuts:
        drawn = drawn * steps_of(stream_key, extent, cuts, -0.22, 0.18)
    return jnp.clip(strengthened(drawn, jax.random.fold_in(stream_key, 3), *heavy), -limit, limit).astype(kind)


def setup_inputs(seed: int = 0) -> dict:
    key_of = jax.random.split(jax.random.key(seed), 7)
    inputs = bell_draw_with(key_of[0], (TOKENS, D), 1.0, 6.0, ((0, 32),), (0, 1, 32, 2.75))
    norm_gain = jnp.clip(1.0 + 0.1 * jax.random.normal(key_of[1], (D,), jnp.float32), 0.5, 1.5).astype(jnp.bfloat16)
    cotangent = normal_values(key_of[2], (TOKENS, FB), 1.0, 6.0, ((0, 32),))
    weights = normal_values(key_of[3], (D, FB), 1.0, 6.0, ((0, 8), (1, 4)))
    first_moment = normal_values(key_of[4], (D, FB), 3.0, 18.0, ((0, 8), (1, 4)))
    second_moment = jnp.clip(jnp.exp(math.log(30.0) - 3.4011974 * jax.random.uniform(key_of[5], (D, FB), jnp.float32) ** steps_of(key_of[5], (D, FB), ((0, 8), (1, 4)), -0.2, 0.2)), 1.0, 30.0).astype(jnp.bfloat16)
    return dict(inputs=inputs, norm_gain=norm_gain, cotangent=cotangent, weights=weights, first_moment=first_moment, second_moment=second_moment)


def reference(inputs, norm_gain, cotangent, weights, first_moment, second_moment):
    factor = D ** (-0.5)
    group = min(64, DEVICES)
    block = TOK_DEV * group
    count = TOKENS // block
    gain_full = norm_gain.astype(jnp.float32)

    def advance(carry, index):
        grad, gain_sum = carry
        start = (index * block).astype(jnp.int32)
        rows = lax.dynamic_slice_in_dim(inputs, start, block, 0).astype(jnp.float32)
        tangent = lax.dynamic_slice_in_dim(cotangent, start, block, 0)
        inverse = lax.rsqrt(lax.optimization_barrier(jnp.mean(rows * rows, axis=1, keepdims=True)) + 1e-05)
        scaled = rows * inverse
        normed = (scaled * gain_full).astype(jnp.bfloat16)
        projected = (factor * jnp.dot(normed, weights, preferred_element_type=jnp.float32)).astype(jnp.bfloat16)
        back = factor * jnp.dot(tangent, weights.T, preferred_element_type=jnp.float32)
        gain_sum = gain_sum + lax.optimization_barrier(jnp.sum(back * scaled, axis=0))

        def per_device(total, pair):
            normed_dev, tangent_dev = pair
            term = (factor * jnp.dot(normed_dev.T, tangent_dev, preferred_element_type=jnp.float32)).astype(jnp.bfloat16)
            term = lax.optimization_barrier(term)
            return (total + term.astype(jnp.float32), None)
        grad, _ = lax.scan(per_device, grad, (normed.reshape(group, TOK_DEV, D), tangent.reshape(group, TOK_DEV, FB)))
        return ((grad, gain_sum), projected)
    start_carry = (jnp.zeros((D, FB), jnp.float32), jnp.zeros((D,), jnp.float32))
    (grad, gain_grad), pieces = lax.scan(advance, start_carry, jnp.arange(count, dtype=jnp.int32))
    projected = pieces.reshape(TOKENS, FB)
    first = 0.9 * first_moment.astype(jnp.float32) + 0.1 * grad
    second = 0.95 * second_moment.astype(jnp.float32) + 0.05 * grad * grad
    update = first / (1.0 - 0.9 ** STEP) / (jnp.sqrt(second / (1.0 - 0.95 ** STEP)) + 1e-08)
    new_weights = (weights.astype(jnp.float32) - 0.05 * update).astype(jnp.bfloat16)
    return (projected, gain_grad, new_weights, first.astype(jnp.bfloat16), second.astype(jnp.bfloat16))
```

```python
import functools

import jax
import jax.numpy as jnp
from jax import lax
from jax.experimental import pallas as pl
from jax.experimental.pallas import tpu as pltpu
from jax.sharding import PartitionSpec as P

STEP = 20
MESH = pl.DeviceIdType.MESH
F32 = jnp.float32
BF16 = jnp.bfloat16


def adam(grad, weights, first_moment, second_moment):
    first = 0.9 * first_moment.astype(F32) + 0.1 * grad
    second = 0.95 * second_moment.astype(F32) + 0.05 * grad * grad
    update = first / (1.0 - 0.9**STEP) / (jnp.sqrt(second / (1.0 - 0.95**STEP)) + 1e-08)
    new_weights = (weights.astype(F32) - 0.05 * update).astype(BF16)
    return new_weights, first.astype(BF16), second.astype(BF16)


def plain(inputs, norm_gain, cotangent, weights, first_moment, second_moment):
    width = inputs.shape[1]
    factor = width ** (-0.5)
    rows_in = inputs.astype(F32)
    inverse = lax.rsqrt(jnp.mean(rows_in * rows_in, axis=1, keepdims=True) + 1e-05)
    scaled = rows_in * inverse
    normed = (scaled * norm_gain.astype(F32)).astype(BF16)
    secondary = lax.all_gather(weights, "dp", axis=0, tiled=True)
    whole = lax.all_gather(secondary, "node", axis=1, tiled=True)
    projected = (factor * jnp.dot(normed, whole, preferred_element_type=F32)).astype(BF16)
    back = factor * lax.dot_general(
        cotangent, whole, (((1,), (1,)), ((), ())), preferred_element_type=F32
    )
    gain_grad = lax.psum(jnp.sum(back * scaled, axis=0), ("dp", "node"))
    raw = factor * lax.dot_general(
        normed, cotangent, (((0,), (0,)), ((), ())), preferred_element_type=F32
    )
    rounded = lax.optimization_barrier(raw.astype(BF16))
    row_sums = lax.psum_scatter(rounded.astype(F32), "dp", scatter_dimension=0, tiled=True)
    grad = lax.psum_scatter(row_sums.astype(BF16), "node", scatter_dimension=1, tiled=True).astype(F32)
    return (projected, gain_grad) + adam(grad, weights, first_moment, second_moment)


def kernel(
    nz, x_ref, gain_ref, cot_ref, w_ref, m1_ref, m2_ref,
    proj_ref, gg_ref, nw_ref, n1_ref, n2_ref,
    G, T, RC, S1, RY, XS, RX, ZS, RZ, OWN, NORM, RSTD, ACC, GA, GB, GR, GZ,
    gy_s, gy_r, gz_s, gz_r, gx_s, gx_r, gc_s, gc_r,
    rc_s, rc_r, ry_s, ry_r, rx_s, rx_r, rz_s, rz_r, ga_s, ga_r,
):
    tok, width = x_ref.shape
    cols, rows = w_ref.shape
    factor = width ** (-0.5)
    chunks = 2 * nz
    dp, node = lax.axis_index("dp"), lax.axis_index("node")
    z, x = dp // 2, lax.rem(dp, 2)
    y, c = node // 2, lax.rem(node, 2)
    core_dev = (dp, y * 2 + 1 - c)
    y_dev = (dp, (1 - y) * 2 + c)
    x_dev = (z * 2 + 1 - x, node)
    z_to = [lax.rem(z + 1 + j, nz) for j in range(nz)]
    z_from = [lax.rem(z + nz - 1 - j, nz) for j in range(nz)]
    z_dev = [(z_to[j] * 2 + x, node) for j in range(nz - 1)]

    sends = []

    def copy(src, dst, s, r, dev):
        return pltpu.make_async_remote_copy(
            src_ref=src, dst_ref=dst, send_sem=s, recv_sem=r, device_id=dev, device_id_type=MESH
        )

    def send(*a):
        d = copy(*a)
        d.start()
        sends.append(d)

    def arrived(dst, s, r, dev):
        copy(dst, dst, s, r, dev).wait_recv()

    barrier = pltpu.get_barrier_semaphore()
    partners = [core_dev, y_dev, x_dev] + z_dev
    for dev in partners:
        pl.semaphore_signal(barrier, inc=1, device_id=dev, device_id_type=MESH)
    pl.semaphore_wait(barrier, len(partners))

    send(w_ref, G.at[c, x, z, y], gy_s, gy_r, y_dev)
    G[c, x, z, y] = w_ref[...]

    square = jnp.zeros((tok, 128), F32)
    for k in range(width // 128):
        v = x_ref[:, k * 128 : (k + 1) * 128].astype(F32)
        square = square + v * v
    RSTD[...] = lax.rsqrt(jnp.sum(square, axis=1, keepdims=True) / width + 1e-05)

    arrived(G.at[c, x, z, 1 - y], gy_s, gy_r, y_dev)
    mine = G.at[c, x, z]
    for j in reversed(range(nz - 1)):
        send(mine, mine, gz_s.at[j], gz_r.at[j], z_dev[j])
    send(mine, mine, gx_s.at[nz - 1], gx_r.at[nz - 1], x_dev)
    send(mine, mine, gc_s.at[nz - 1], gc_r.at[nz - 1], core_dev)

    half = 2 * cols
    a = lax.broadcasted_iota(jnp.int32, (4 * cols, 4 * cols), 0)
    b = lax.broadcasted_iota(jnp.int32, (4 * cols, 4 * cols), 1)
    source = (lax.rem(b, half) // cols) * half + (b // half) * cols + lax.rem(b, cols)
    perm = jnp.where(a == source, 1.0, 0.0).astype(BF16)
    cot = jnp.dot(cot_ref[...], perm, preferred_element_type=F32).astype(BF16)
    cot_t = cot.T

    def place(k):
        xk = 1 - x if k < nz else x
        return xk, z_to[k % nz]

    def lanes(xk, zk):
        return pl.ds(pl.multiple_of((zk * 2 + xk) * rows, 128), rows)

    def stage_term(k):
        xk, zk = place(k)
        at = lanes(xk, zk)
        scaled = x_ref[:, at].astype(F32) * RSTD[...]
        normed = (scaled * gain_ref[:, at].astype(F32)).astype(BF16)
        NORM[zk * 2 + xk] = normed
        term = (factor * jnp.dot(cot_t, normed, preferred_element_type=F32)).astype(BF16)
        T[k, 0] = term[:half].reshape(2, cols, rows)
        T[k, 1] = term[half:].reshape(2, cols, rows)
        send(T.at[k, 1 - c], RC.at[k], rc_s.at[k], rc_r.at[k], core_dev)

    def stage_core(k):
        arrived(RC.at[k], rc_s.at[k], rc_r.at[k], core_dev)
        S1[k] = (T[k, c].astype(F32) + RC[k].astype(F32)).astype(BF16)
        send(S1.at[k, 1 - y], RY.at[k], ry_s.at[k], ry_r.at[k], y_dev)

    def stage_y(k):
        arrived(RY.at[k], ry_s.at[k], ry_r.at[k], y_dev)
        total = S1[k, y].astype(F32) + RY[k].astype(F32)
        if k < nz:
            XS[k] = total.astype(BF16)
            send(XS.at[k], RX.at[k], rx_s.at[k], rx_r.at[k], x_dev)
            return
        j = k - nz
        arrived(RX.at[j], rx_s.at[j], rx_r.at[j], x_dev)
        total = total + RX[j].astype(F32)
        if j < nz - 1:
            ZS[j] = total.astype(BF16)
            send(ZS.at[j], RZ.at[j], rz_s.at[j], rz_r.at[j], z_dev[j])
        else:
            OWN[...] = total

    def forward_z(j):
        block = G.at[c, x, z_from[j]]
        arrived(block, gz_s.at[j], gz_r.at[j], z_dev[j])
        send(block, block, gx_s.at[j], gx_r.at[j], x_dev)
        send(block, block, gc_s.at[j], gc_r.at[j], core_dev)

    def forward_x(j):
        block = G.at[c, 1 - x, z_from[j]]
        arrived(block, gx_s.at[j], gx_r.at[j], x_dev)
        send(block, block, gc_s.at[nz + j], gc_r.at[nz + j], core_dev)

    def use(i):
        j = i % nz
        xk, zk = (x if i < nz else 1 - x), z_from[j]
        arrived(G.at[1 - c, xk, zk], gc_s.at[i], gc_r.at[i], core_dev)
        at = lanes(xk, zk)
        wt = jnp.concatenate(
            [G[0, xk, zk].reshape(half, rows), G[1, xk, zk].reshape(half, rows)], axis=0
        )
        part = lax.dot_general(
            NORM[zk * 2 + xk], wt, (((1,), (1,)), ((), ())), preferred_element_type=F32
        )
        ACC[...] += part
        back = factor * jnp.dot(cot, wt, preferred_element_type=F32)
        scaled = x_ref[:, at].astype(F32) * RSTD[...]
        GA[pl.ds(zk * 2 + xk, 1), :] = jnp.sum(back * scaled, axis=0, keepdims=True)

    ACC[...] = jnp.zeros_like(ACC)
    for k in range(chunks):
        stage_term(k)
        if k >= 1:
            stage_core(k - 1)
    stage_core(chunks - 1)
    stage_y(0)
    stage_y(1)
    use(nz - 1)
    forward_x(nz - 1)
    done = 2
    for j in reversed(range(nz - 1)):
        stage_y(done)
        forward_z(j)
        use(nz + nz - 1) if j == nz - 2 else forward_x(j + 1)
        done += 1
    for j in reversed(range(nz - 1)):
        if done < chunks:
            stage_y(done)
            done += 1
        use(j)
    forward_x(0)
    while done < chunks:
        stage_y(done)
        done += 1
    for j in reversed(range(nz - 1)):
        use(nz + j)

    send(GA, GR.at[0], ga_s.at[0], ga_r.at[0], core_dev)
    out = lax.dot_general(
        (factor * ACC[...]).astype(BF16), perm, (((1,), (1,)), ((), ())), preferred_element_type=F32
    )
    proj_ref[...] = out.astype(BF16)
    arrived(GR.at[0], ga_s.at[0], ga_r.at[0], core_dev)
    GB[0] = GA[...] + GR[0]
    send(GB.at[0], GR.at[1], ga_s.at[1], ga_r.at[1], y_dev)
    arrived(GR.at[1], ga_s.at[1], ga_r.at[1], y_dev)
    GB[1] = GB[0] + GR[1]
    send(GB.at[1], GR.at[2], ga_s.at[2], ga_r.at[2], x_dev)
    arrived(GR.at[2], ga_s.at[2], ga_r.at[2], x_dev)
    GZ[z] = GB[1] + GR[2]
    for j in range(nz - 1):
        send(GZ.at[z], GZ.at[z], ga_s.at[3 + j], ga_r.at[3 + j], z_dev[j])

    grad = OWN[...]
    for j in range(nz - 1):
        arrived(RZ.at[j], rz_s.at[j], rz_r.at[j], z_dev[j])
        grad = grad + RZ[j].astype(F32)
    nw_ref[...], n1_ref[...], n2_ref[...] = adam(grad, w_ref[...], m1_ref[...], m2_ref[...])

    for j in range(nz - 1):
        arrived(GZ.at[z_from[j]], ga_s.at[3 + j], ga_r.at[3 + j], z_dev[j])
    total = GZ[0]
    for j in range(1, nz):
        total = total + GZ[j]
    gg_ref[...] = total
    for d in sends:
        d.wait_send()


def per_device(nz, inputs, norm_gain, cotangent, weights, first_moment, second_moment):
    tok, width = inputs.shape
    rows, cols = weights.shape
    chunks = 2 * nz
    vm = pl.BlockSpec(memory_space=pltpu.VMEM)
    dma = lambda *n: pltpu.SemaphoreType.DMA(n)
    sd = jax.ShapeDtypeStruct
    block = (cols, rows)
    outs = pl.pallas_call(
        functools.partial(kernel, nz),
        out_shape=(
            sd((tok, 4 * cols), BF16),
            sd((chunks, rows), F32),
            sd(block, BF16),
            sd(block, BF16),
            sd(block, BF16),
        ),
        in_specs=[vm] * 6,
        out_specs=(vm,) * 5,
        scratch_shapes=[
            pltpu.VMEM((2, 2, nz, 2) + block, BF16),
            pltpu.VMEM((chunks, 2, 2) + block, BF16),
            pltpu.VMEM((chunks, 2) + block, BF16),
            pltpu.VMEM((chunks, 2) + block, BF16),
            pltpu.VMEM((chunks,) + block, BF16),
            pltpu.VMEM((nz,) + block, BF16),
            pltpu.VMEM((nz,) + block, BF16),
            pltpu.VMEM((nz - 1,) + block, BF16),
            pltpu.VMEM((nz - 1,) + block, BF16),
            pltpu.VMEM(block, F32),
            pltpu.VMEM((chunks, tok, rows), BF16),
            pltpu.VMEM((tok, 1), F32),
            pltpu.VMEM((tok, 4 * cols), F32),
            pltpu.VMEM((chunks, rows), F32),
            pltpu.VMEM((2, chunks, rows), F32),
            pltpu.VMEM((3, chunks, rows), F32),
            pltpu.VMEM((nz, chunks, rows), F32),
            pltpu.SemaphoreType.DMA, pltpu.SemaphoreType.DMA,
            dma(nz - 1), dma(nz - 1), dma(nz), dma(nz), dma(chunks), dma(chunks),
            dma(chunks), dma(chunks), dma(chunks), dma(chunks),
            dma(nz), dma(nz), dma(nz - 1), dma(nz - 1), dma(nz + 2), dma(nz + 2),
        ],
        compiler_params=pltpu.CompilerParams(
            collective_id=0, has_side_effects=True, vmem_limit_bytes=56 * 2**20
        ),
    )(inputs, norm_gain.reshape(1, width), cotangent, weights.T, first_moment.T, second_moment.T)
    projected, gain_grad, new_weights, first, second = outs
    return projected, gain_grad.reshape(width), new_weights.T, first.T, second.T


def solution(mesh):
    dp, node = mesh.shape["dp"], mesh.shape["node"]

    def body(inputs, norm_gain, cotangent, weights, first_moment, second_moment):
        args = (inputs, norm_gain, cotangent, weights, first_moment, second_moment)
        rows, cols = weights.shape
        if node == 4 and dp in (4, 6, 8) and rows % 128 == 0 and cols % 16 == 0:
            return per_device(dp // 2, *args)
        return plain(*args)

    return jax.shard_map(
        body,
        mesh=mesh,
        in_specs=(
            P(("dp", "node"), None),
            P(),
            P(("dp", "node"), None),
            P("dp", "node"),
            P("dp", "node"),
            P("dp", "node"),
        ),
        out_specs=(P(("dp", "node"), None), P(), P("dp", "node"), P("dp", "node"), P("dp", "node")),
        check_vma=False,
    )
```

```python
import functools

import jax
import jax.numpy as jnp
from jax import lax
from jax.experimental import pallas as pl
from jax.experimental.pallas import tpu as pltpu
from jax.sharding import PartitionSpec as P

STEP = 20
ORDER = "yzxc"
PLAN = "TTCP" + "TCYP" * 6 + "CP" + "YPPP" * 8
MESH = pl.DeviceIdType.MESH
F32 = jnp.float32
BF16 = jnp.bfloat16


def adam(grad, weights, first_moment, second_moment):
    first = 0.9 * first_moment.astype(F32) + 0.1 * grad
    second = 0.95 * second_moment.astype(F32) + 0.05 * grad * grad
    update = first / (1.0 - 0.9**STEP) / (jnp.sqrt(second / (1.0 - 0.95**STEP)) + 1e-08)
    new_weights = (weights.astype(F32) - 0.05 * update).astype(BF16)
    return new_weights, first.astype(BF16), second.astype(BF16)


def plain(inputs, norm_gain, cotangent, weights, first_moment, second_moment):
    width = inputs.shape[1]
    factor = width ** (-0.5)
    rows_in = inputs.astype(F32)
    inverse = lax.rsqrt(jnp.mean(rows_in * rows_in, axis=1, keepdims=True) + 1e-05)
    scaled = rows_in * inverse
    normed = (scaled * norm_gain.astype(F32)).astype(BF16)
    secondary = lax.all_gather(weights, "dp", axis=0, tiled=True)
    whole = lax.all_gather(secondary, "node", axis=1, tiled=True)
    projected = (factor * jnp.dot(normed, whole, preferred_element_type=F32)).astype(BF16)
    back = factor * lax.dot_general(
        cotangent, whole, (((1,), (1,)), ((), ())), preferred_element_type=F32
    )
    gain_grad = lax.psum(jnp.sum(back * scaled, axis=0), ("dp", "node"))
    raw = factor * lax.dot_general(
        normed, cotangent, (((0,), (0,)), ((), ())), preferred_element_type=F32
    )
    rounded = lax.optimization_barrier(raw.astype(BF16))
    row_sums = lax.psum_scatter(rounded.astype(F32), "dp", scatter_dimension=0, tiled=True)
    grad = lax.psum_scatter(row_sums.astype(BF16), "node", scatter_dimension=1, tiled=True).astype(F32)
    return (projected, gain_grad) + adam(grad, weights, first_moment, second_moment)


def kernel(
    nz, x_ref, gain_ref, cot_ref, w_ref,
    proj_ref, gg_ref, grad_ref,
    GF, G, T, RC, S1, RY, XS, RX, ZS, RZ, OWN, NORM, RSTD, ACC, GA, GB, GR, GZ,
    g_s, g_r,
    rc_s, rc_r, ry_s, ry_r, rx_s, rx_r, rz_s, rz_r, ga_s, ga_r, gt_s, gt_r, gb_s, gb_r,
):
    tok, width = x_ref.shape
    cols, rows = w_ref.shape
    factor = width ** (-0.5)
    chunks = 2 * nz
    dp, node = lax.axis_index("dp"), lax.axis_index("node")
    z, x = dp // 2, lax.rem(dp, 2)
    y, c = node // 2, lax.rem(node, 2)
    core_dev = (dp, y * 2 + 1 - c)
    y_dev = (dp, (1 - y) * 2 + c)
    x_dev = (z * 2 + 1 - x, node)
    z_to = [lax.rem(z + 1 + j, nz) for j in range(nz)]
    z_from = [lax.rem(z + nz - 1 - j, nz) for j in range(nz)]
    z_dev = [(z_to[j] * 2 + x, node) for j in range(nz - 1)]

    sends = []

    def copy(src, dst, s, r, dev):
        return pltpu.make_async_remote_copy(
            src_ref=src, dst_ref=dst, send_sem=s, recv_sem=r, device_id=dev, device_id_type=MESH
        )

    def send(*a):
        d = copy(*a)
        d.start()
        sends.append(d)

    def arrived(dst, s, r, dev):
        copy(dst, dst, s, r, dev).wait_recv()

    barrier = pltpu.get_barrier_semaphore()
    group = []
    for q in range(1, 8):
        xq, yq, cq = lax.rem(x + q // 4, 2), lax.rem(y + q // 2 % 2, 2), lax.rem(c + q % 2, 2)
        group.append(((z * 2 + xq, yq * 2 + cq), xq * 4 + yq * 2 + cq))
    partners = [dev for dev, _ in group] + z_dev
    for dev in partners:
        pl.semaphore_signal(barrier, inc=1, device_id=dev, device_id_type=MESH)
    pl.semaphore_wait(barrier, len(partners))

    size = dict(z=nz, x=2, y=2, c=2)
    here = dict(z=z, x=x, y=y, c=c)
    waiting, have = [], {}

    def block(o):
        p = {d: lax.rem(here[d] + o[d], size[d]) for d in size}
        return G.at[p["c"], p["x"], p["z"], p["y"]]

    def hand_on(o, axes, src):
        for i, d in enumerate(axes):
            for j in reversed(range(1, size[d])):
                n = left.pop(0)
                dev = {"z": z_dev[j - 1] if d == "z" else None, "x": x_dev, "y": y_dev, "c": core_dev}[d]
                send(src, block(o), g_s.at[n], g_r.at[n], dev)
                waiting.append((dict(o, **{d: (o[d] - j) % size[d]}), axes[i + 1 :], n, dev))

    left = list(range(4 * chunks - 1))
    zero = dict(z=0, x=0, y=0, c=0)
    hand_on(zero, ORDER, w_ref)
    G[c, x, z, y] = w_ref[...]
    have[0, 0] = 1
    gains = gain_ref[...].astype(F32)
    for r in range(width // 128):
        GF[:, r * 128 : (r + 1) * 128] = gains[r : r + 1, :]

    square = jnp.zeros((tok, 128), F32)
    for k in range(width // 128):
        v = x_ref[:, k * 128 : (k + 1) * 128].astype(F32)
        square = square + v * v
    RSTD[...] = lax.rsqrt(jnp.sum(square, axis=1, keepdims=True) / width + 1e-05)

    half = 2 * cols
    a = lax.broadcasted_iota(jnp.int32, (4 * cols, 4 * cols), 0)
    b = lax.broadcasted_iota(jnp.int32, (4 * cols, 4 * cols), 1)
    source = (lax.rem(b, half) // cols) * half + (b // half) * cols + lax.rem(b, cols)
    perm = jnp.where(a == source, 1.0, 0.0).astype(BF16)
    cot = jnp.dot(cot_ref[...], perm, preferred_element_type=F32).astype(BF16)
    cot_t = cot.T

    def place(k):
        xk = 1 - x if k < nz else x
        return xk, z_to[k % nz]

    def lanes(xk, zk):
        return pl.ds(pl.multiple_of((zk * 2 + xk) * rows, 128), rows)

    def stage_term(k):
        xk, zk = place(k)
        at = lanes(xk, zk)
        scaled = x_ref[:, at].astype(F32) * RSTD[...]
        normed = (scaled * GF[:, at]).astype(BF16)
        NORM[zk * 2 + xk] = normed
        term = (factor * jnp.dot(cot_t, normed, preferred_element_type=F32)).astype(BF16)
        T[k, 0] = term[:half].reshape(2, cols, rows)
        T[k, 1] = term[half:].reshape(2, cols, rows)
        send(T.at[k, 1 - c], RC.at[k], rc_s.at[k], rc_r.at[k], core_dev)

    def stage_core(k):
        arrived(RC.at[k], rc_s.at[k], rc_r.at[k], core_dev)
        S1[k] = (T[k, c].astype(F32) + RC[k].astype(F32)).astype(BF16)
        send(S1.at[k, 1 - y], RY.at[k], ry_s.at[k], ry_r.at[k], y_dev)

    def stage_y(k):
        arrived(RY.at[k], ry_s.at[k], ry_r.at[k], y_dev)
        total = S1[k, y].astype(F32) + RY[k].astype(F32)
        if k < nz:
            XS[k] = total.astype(BF16)
            send(XS.at[k], RX.at[k], rx_s.at[k], rx_r.at[k], x_dev)
            return
        j = k - nz
        arrived(RX.at[j], rx_s.at[j], rx_r.at[j], x_dev)
        total = total + RX[j].astype(F32)
        if j < nz - 1:
            ZS[j] = total.astype(BF16)
            send(ZS.at[j], RZ.at[j], rz_s.at[j], rz_r.at[j], z_dev[j])
        else:
            OWN[...] = total

    def pump():
        o, axes, n, dev = waiting.pop(0)
        arrived(block(o), g_s.at[n], g_r.at[n], dev)
        hand_on(o, axes, block(o))
        key = o["x"], o["z"]
        have[key] = have.get(key, 0) + 1
        if have[key] == 4:
            use(lax.rem(x + key[0], 2), lax.rem(z + key[1], nz))

    def use(xk, zk):
        at = lanes(xk, zk)
        wt = jnp.concatenate(
            [G[0, xk, zk].reshape(half, rows), G[1, xk, zk].reshape(half, rows)], axis=0
        )
        part = lax.dot_general(
            NORM[zk * 2 + xk], wt, (((1,), (1,)), ((), ())), preferred_element_type=F32
        )
        ACC[...] += part
        back = factor * jnp.dot(cot, wt, preferred_element_type=F32)
        scaled = x_ref[:, at].astype(F32) * RSTD[...]
        GA[zk * 2 + xk] = jnp.sum(back * scaled, axis=0, keepdims=True)

    ACC[...] = jnp.zeros_like(ACC)
    count = dict(T=0, C=0, Y=0)
    stages = dict(T=stage_term, C=stage_core, Y=stage_y)
    for letter in PLAN + "P" * (4 * chunks) + "TTTTCCCCYYYY" * 2:
        if letter == "P":
            if waiting:
                pump()
        elif count[letter] < chunks:
            stages[letter](count[letter])
            count[letter] += 1

    row = x * 4 + y * 2 + c
    for q, (dev, other) in enumerate(group):
        send(GA.at[other], GR.at[q], ga_s.at[q], ga_r.at[q], dev)
    out = lax.dot_general(
        (factor * ACC[...]).astype(BF16), perm, (((1,), (1,)), ((), ())), preferred_element_type=F32
    )
    proj_ref[...] = out.astype(BF16)
    part = GA[row]
    for q, (dev, _) in enumerate(group):
        arrived(GR.at[q], ga_s.at[q], ga_r.at[q], dev)
        part = part + GR[q]
    GZ[z] = part
    for j in range(nz - 1):
        send(GZ.at[z], GZ.at[z], gt_s.at[j], gt_r.at[j], z_dev[j])

    grad = OWN[...]
    for j in range(nz - 1):
        arrived(RZ.at[j], rz_s.at[j], rz_r.at[j], z_dev[j])
        grad = grad + RZ[j].astype(F32)
    grad_ref[...] = grad

    for j in range(nz - 1):
        arrived(GZ.at[z_from[j]], gt_s.at[j], gt_r.at[j], z_dev[j])
    total = GZ[0]
    for j in range(1, nz):
        total = total + GZ[j]
    GB[row] = total
    for q, (dev, _) in enumerate(group):
        send(GB.at[row], GB.at[row], gb_s.at[q], gb_r.at[q], dev)
    for q, (dev, other) in enumerate(group):
        arrived(GB.at[other], gb_s.at[q], gb_r.at[q], dev)
    for r in range(chunks):
        gg_ref[r : r + 1, :] = GB[r]
    for d in sends:
        d.wait_send()


def finish(p_ref, g_ref, grad_ref, w_ref, m1_ref, m2_ref, proj_ref, gg_ref, nw_ref, n1_ref, n2_ref):
    proj_ref[...] = p_ref[...]
    per = g_ref.shape[1] // 128
    for r in range(gg_ref.shape[0]):
        at = (r % per) * 128
        gg_ref[r : r + 1, :] = g_ref[r // per : r // per + 1, at : at + 128]
    nw_ref[...], n1_ref[...], n2_ref[...] = adam(
        grad_ref[...], w_ref[...], m1_ref[...], m2_ref[...]
    )


def per_device(nz, inputs, norm_gain, cotangent, weights, first_moment, second_moment):
    tok, width = inputs.shape
    rows, cols = weights.shape
    chunks = 2 * nz
    vm = pl.BlockSpec(memory_space=pltpu.VMEM)
    dma = lambda *n: pltpu.SemaphoreType.DMA(n)
    sd = jax.ShapeDtypeStruct
    block = (cols, rows)
    weights, first_moment, second_moment = weights.T, first_moment.T, second_moment.T
    projected, gains, grad = pl.pallas_call(
        functools.partial(kernel, nz),
        out_shape=(sd((tok, 4 * cols), BF16), sd((chunks, rows), F32), sd(block, F32)),
        in_specs=[vm] * 4,
        out_specs=(vm,) * 3,
        scratch_shapes=[
            pltpu.VMEM((1, width), F32),
            pltpu.VMEM((2, 2, nz, 2) + block, BF16),
            pltpu.VMEM((chunks, 2, 2) + block, BF16),
            pltpu.VMEM((chunks, 2) + block, BF16),
            pltpu.VMEM((chunks, 2) + block, BF16),
            pltpu.VMEM((chunks,) + block, BF16),
            pltpu.VMEM((nz,) + block, BF16),
            pltpu.VMEM((nz,) + block, BF16),
            pltpu.VMEM((nz - 1,) + block, BF16),
            pltpu.VMEM((nz - 1,) + block, BF16),
            pltpu.VMEM(block, F32),
            pltpu.VMEM((chunks, tok, rows), BF16),
            pltpu.VMEM((tok, 1), F32),
            pltpu.VMEM((tok, 4 * cols), F32),
            pltpu.VMEM((chunks, 1, rows), F32),
            pltpu.VMEM((chunks, 1, rows), F32),
            pltpu.VMEM((7, 1, rows), F32),
            pltpu.VMEM((nz, 1, rows), F32),
            dma(4 * chunks - 1), dma(4 * chunks - 1),
            dma(chunks), dma(chunks), dma(chunks), dma(chunks),
            dma(nz), dma(nz), dma(nz - 1), dma(nz - 1), dma(7), dma(7),
            dma(nz - 1), dma(nz - 1), dma(7), dma(7),
        ],
        compiler_params=pltpu.CompilerParams(
            collective_id=0, has_side_effects=True, vmem_limit_bytes=56 * 2**20
        ),
    )(inputs, norm_gain.reshape(width // 128, 128), cotangent, weights)
    projected, gain_grad, new_weights, first, second = pl.pallas_call(
        finish,
        out_shape=(
            sd((tok, 4 * cols), BF16), sd((width // 128, 128), F32),
            sd(block, BF16), sd(block, BF16), sd(block, BF16),
        ),
        in_specs=[vm] * 6,
        out_specs=(vm,) * 5,
    )(projected, gains, grad, weights, first_moment, second_moment)
    return projected, gain_grad.reshape(width), new_weights.T, first.T, second.T


def solution(mesh):
    dp, node = mesh.shape["dp"], mesh.shape["node"]

    def body(inputs, norm_gain, cotangent, weights, first_moment, second_moment):
        args = (inputs, norm_gain, cotangent, weights, first_moment, second_moment)
        rows, cols = weights.shape
        if node == 4 and dp == 8 and rows % 128 == 0 and cols % 16 == 0:
            return per_device(dp // 2, *args)
        return plain(*args)

    return jax.shard_map(
        body,
        mesh=mesh,
        in_specs=(
            P(("dp", "node"), None),
            P(),
            P(("dp", "node"), None),
            P("dp", "node"),
            P("dp", "node"),
            P("dp", "node"),
        ),
        out_specs=(P(("dp", "node"), None), P(), P("dp", "node"), P("dp", "node"), P("dp", "node")),
        check_vma=False,
    )
```

```python
import functools

import jax
import jax.numpy as jnp
from jax import lax
from jax.experimental import pallas as pl
from jax.experimental.pallas import tpu as pltpu
from jax.sharding import PartitionSpec as P

STEP = 20
ORDER = "yzxc"
PLAN = "PTTC" + "TCYP" * 6 + "CP" + "YPPP" * 8
MESH = pl.DeviceIdType.MESH
F32 = jnp.float32
BF16 = jnp.bfloat16


def adam(grad, weights, first_moment, second_moment):
    first = 0.9 * first_moment.astype(F32) + 0.1 * grad
    second = 0.95 * second_moment.astype(F32) + 0.05 * grad * grad
    update = first / (1.0 - 0.9**STEP) / (jnp.sqrt(second / (1.0 - 0.95**STEP)) + 1e-08)
    new_weights = (weights.astype(F32) - 0.05 * update).astype(BF16)
    return new_weights, first.astype(BF16), second.astype(BF16)


def plain(inputs, norm_gain, cotangent, weights, first_moment, second_moment):
    width = inputs.shape[1]
    factor = width ** (-0.5)
    rows_in = inputs.astype(F32)
    inverse = lax.rsqrt(jnp.mean(rows_in * rows_in, axis=1, keepdims=True) + 1e-05)
    scaled = rows_in * inverse
    normed = (scaled * norm_gain.astype(F32)).astype(BF16)
    secondary = lax.all_gather(weights, "dp", axis=0, tiled=True)
    whole = lax.all_gather(secondary, "node", axis=1, tiled=True)
    projected = (factor * jnp.dot(normed, whole, preferred_element_type=F32)).astype(BF16)
    back = factor * lax.dot_general(
        cotangent, whole, (((1,), (1,)), ((), ())), preferred_element_type=F32
    )
    gain_grad = lax.psum(jnp.sum(back * scaled, axis=0), ("dp", "node"))
    raw = factor * lax.dot_general(
        normed, cotangent, (((0,), (0,)), ((), ())), preferred_element_type=F32
    )
    rounded = lax.optimization_barrier(raw.astype(BF16))
    row_sums = lax.psum_scatter(rounded.astype(F32), "dp", scatter_dimension=0, tiled=True)
    grad = lax.psum_scatter(row_sums.astype(BF16), "node", scatter_dimension=1, tiled=True).astype(F32)
    return (projected, gain_grad) + adam(grad, weights, first_moment, second_moment)


def kernel(
    nz, x_ref, gain_ref, cot_ref, w_ref,
    proj_ref, gg_ref, grad_ref,
    GF, G, T, RC, S1, RY, XS, RX, ZS, RZ, OWN, NORM, RSTD, ACC, GA, GB, GR, GZ,
    g_s, g_r,
    rc_s, rc_r, ry_s, ry_r, rx_s, rx_r, rz_s, rz_r, ga_s, ga_r, gt_s, gt_r, gb_s, gb_r,
):
    tok, width = x_ref.shape
    cols, rows = w_ref.shape
    factor = width ** (-0.5)
    chunks = 2 * nz
    dp, node = lax.axis_index("dp"), lax.axis_index("node")
    z, x = dp // 2, lax.rem(dp, 2)
    y, c = node // 2, lax.rem(node, 2)
    core_dev = (dp, y * 2 + 1 - c)
    y_dev = (dp, (1 - y) * 2 + c)
    x_dev = (z * 2 + 1 - x, node)
    z_to = [lax.rem(z + 1 + j, nz) for j in range(nz)]
    z_from = [lax.rem(z + nz - 1 - j, nz) for j in range(nz)]
    z_dev = [(z_to[j] * 2 + x, node) for j in range(nz - 1)]

    sends = []

    def copy(src, dst, s, r, dev):
        return pltpu.make_async_remote_copy(
            src_ref=src, dst_ref=dst, send_sem=s, recv_sem=r, device_id=dev, device_id_type=MESH
        )

    def send(*a):
        d = copy(*a)
        d.start()
        sends.append(d)

    def arrived(dst, s, r, dev):
        copy(dst, dst, s, r, dev).wait_recv()

    barrier = pltpu.get_barrier_semaphore()
    group = []
    for q in range(1, 8):
        xq, yq, cq = lax.rem(x + q // 4, 2), lax.rem(y + q // 2 % 2, 2), lax.rem(c + q % 2, 2)
        group.append(((z * 2 + xq, yq * 2 + cq), xq * 4 + yq * 2 + cq))
    partners = [dev for dev, _ in group] + z_dev
    for dev in partners:
        pl.semaphore_signal(barrier, inc=1, device_id=dev, device_id_type=MESH)
    pl.semaphore_wait(barrier, len(partners))

    size = dict(z=nz, x=2, y=2, c=2)
    here = dict(z=z, x=x, y=y, c=c)
    waiting, have = [], {}

    def block(o):
        p = {d: lax.rem(here[d] + o[d], size[d]) for d in size}
        return G.at[p["c"], p["x"], p["z"], p["y"]]

    def hand_on(o, axes, src):
        for i, d in enumerate(axes):
            for j in reversed(range(1, size[d])):
                n = left.pop(0)
                dev = {"z": z_dev[j - 1] if d == "z" else None, "x": x_dev, "y": y_dev, "c": core_dev}[d]
                send(src, block(o), g_s.at[n], g_r.at[n], dev)
                waiting.append((dict(o, **{d: (o[d] - j) % size[d]}), axes[i + 1 :], n, dev))

    left = list(range(4 * chunks - 1))
    zero = dict(z=0, x=0, y=0, c=0)
    hand_on(zero, ORDER, w_ref)
    G[c, x, z, y] = w_ref[...]
    have[0, 0] = 1
    gains = gain_ref[...].astype(F32)
    for r in range(width // 128):
        GF[:, r * 128 : (r + 1) * 128] = gains[r : r + 1, :]

    square = jnp.zeros((tok, 128), F32)
    for k in range(width // 128):
        v = x_ref[:, k * 128 : (k + 1) * 128].astype(F32)
        square = square + v * v
    RSTD[...] = lax.rsqrt(jnp.sum(square, axis=1, keepdims=True) / width + 1e-05)

    half = 2 * cols
    a = lax.broadcasted_iota(jnp.int32, (4 * cols, 4 * cols), 0)
    b = lax.broadcasted_iota(jnp.int32, (4 * cols, 4 * cols), 1)
    source = (lax.rem(b, half) // cols) * half + (b // half) * cols + lax.rem(b, cols)
    perm = jnp.where(a == source, 1.0, 0.0).astype(BF16)
    cot = jnp.dot(cot_ref[...], perm, preferred_element_type=F32).astype(BF16)
    cot_t = cot.T

    def place(k):
        xk = 1 - x if k < nz else x
        return xk, z_to[k % nz]

    def lanes(xk, zk):
        return pl.ds(pl.multiple_of((zk * 2 + xk) * rows, 128), rows)

    def stage_term(k):
        xk, zk = place(k)
        at = lanes(xk, zk)
        scaled = x_ref[:, at].astype(F32) * RSTD[...]
        normed = (scaled * GF[:, at]).astype(BF16)
        NORM[zk * 2 + xk] = normed
        term = (factor * jnp.dot(cot_t, normed, preferred_element_type=F32)).astype(BF16)
        T[k, 0] = term[:half].reshape(2, cols, rows)
        T[k, 1] = term[half:].reshape(2, cols, rows)
        send(T.at[k, 1 - c], RC.at[k], rc_s.at[k], rc_r.at[k], core_dev)

    def stage_core(k):
        arrived(RC.at[k], rc_s.at[k], rc_r.at[k], core_dev)
        S1[k] = (T[k, c].astype(F32) + RC[k].astype(F32)).astype(BF16)
        send(S1.at[k, 1 - y], RY.at[k], ry_s.at[k], ry_r.at[k], y_dev)

    def stage_y(k):
        arrived(RY.at[k], ry_s.at[k], ry_r.at[k], y_dev)
        total = S1[k, y].astype(F32) + RY[k].astype(F32)
        if k < nz:
            XS[k] = total.astype(BF16)
            send(XS.at[k], RX.at[k], rx_s.at[k], rx_r.at[k], x_dev)
            return
        j = k - nz
        arrived(RX.at[j], rx_s.at[j], rx_r.at[j], x_dev)
        total = total + RX[j].astype(F32)
        if j < nz - 1:
            ZS[j] = total.astype(BF16)
            send(ZS.at[j], RZ.at[j], rz_s.at[j], rz_r.at[j], z_dev[j])
        else:
            OWN[...] = total

    def pump():
        o, axes, n, dev = waiting.pop(0)
        arrived(block(o), g_s.at[n], g_r.at[n], dev)
        hand_on(o, axes, block(o))
        key = o["x"], o["z"]
        have[key] = have.get(key, 0) + 1
        if have[key] == 4:
            use(lax.rem(x + key[0], 2), lax.rem(z + key[1], nz))

    def use(xk, zk):
        at = lanes(xk, zk)
        wt = jnp.concatenate(
            [G[0, xk, zk].reshape(half, rows), G[1, xk, zk].reshape(half, rows)], axis=0
        )
        part = lax.dot_general(
            NORM[zk * 2 + xk], wt, (((1,), (1,)), ((), ())), preferred_element_type=F32
        )
        ACC[...] += part
        back = factor * jnp.dot(cot, wt, preferred_element_type=F32)
        scaled = x_ref[:, at].astype(F32) * RSTD[...]
        GA[zk * 2 + xk] = jnp.sum(back * scaled, axis=0, keepdims=True)

    ACC[...] = jnp.zeros_like(ACC)
    count = dict(T=0, C=0, Y=0)
    stages = dict(T=stage_term, C=stage_core, Y=stage_y)
    for letter in PLAN + "P" * (4 * chunks) + "TTTTCCCCYYYY" * 2:
        if letter == "P":
            if waiting:
                pump()
        elif count[letter] < chunks:
            stages[letter](count[letter])
            count[letter] += 1

    row = x * 4 + y * 2 + c
    for q, (dev, other) in enumerate(group):
        send(GA.at[other], GR.at[q], ga_s.at[q], ga_r.at[q], dev)
    out = lax.dot_general(
        (factor * ACC[...]).astype(BF16), perm, (((1,), (1,)), ((), ())), preferred_element_type=F32
    )
    proj_ref[...] = out.astype(BF16)
    part = GA[row]
    for q, (dev, _) in enumerate(group):
        arrived(GR.at[q], ga_s.at[q], ga_r.at[q], dev)
        part = part + GR[q]
    GZ[z] = part
    for j in range(nz - 1):
        send(GZ.at[z], GZ.at[z], gt_s.at[j], gt_r.at[j], z_dev[j])

    grad = OWN[...]
    for j in range(nz - 1):
        arrived(RZ.at[j], rz_s.at[j], rz_r.at[j], z_dev[j])
        grad = grad + RZ[j].astype(F32)
    grad_ref[...] = grad

    for j in range(nz - 1):
        arrived(GZ.at[z_from[j]], gt_s.at[j], gt_r.at[j], z_dev[j])
    total = GZ[0]
    for j in range(1, nz):
        total = total + GZ[j]
    GB[row] = total
    for q, (dev, _) in enumerate(group):
        send(GB.at[row], GB.at[row], gb_s.at[q], gb_r.at[q], dev)
    for q, (dev, other) in enumerate(group):
        arrived(GB.at[other], gb_s.at[q], gb_r.at[q], dev)
    for r in range(chunks):
        gg_ref[r : r + 1, :] = GB[r]
    for d in sends:
        d.wait_send()


def finish(p_ref, g_ref, grad_ref, w_ref, m1_ref, m2_ref, proj_ref, gg_ref, nw_ref, n1_ref, n2_ref):
    proj_ref[...] = p_ref[...]
    per = g_ref.shape[1] // 128
    for r in range(gg_ref.shape[0]):
        at = (r % per) * 128
        gg_ref[r : r + 1, :] = g_ref[r // per : r // per + 1, at : at + 128]
    nw_ref[...], n1_ref[...], n2_ref[...] = adam(
        grad_ref[...], w_ref[...], m1_ref[...], m2_ref[...]
    )


def per_device(nz, inputs, norm_gain, cotangent, weights, first_moment, second_moment):
    tok, width = inputs.shape
    rows, cols = weights.shape
    chunks = 2 * nz
    vm = pl.BlockSpec(memory_space=pltpu.VMEM)
    dma = lambda *n: pltpu.SemaphoreType.DMA(n)
    sd = jax.ShapeDtypeStruct
    block = (cols, rows)
    weights, first_moment, second_moment = weights.T, first_moment.T, second_moment.T
    projected, gains, grad = pl.pallas_call(
        functools.partial(kernel, nz),
        out_shape=(sd((tok, 4 * cols), BF16), sd((chunks, rows), F32), sd(block, F32)),
        in_specs=[vm] * 4,
        out_specs=(vm,) * 3,
        scratch_shapes=[
            pltpu.VMEM((1, width), F32),
            pltpu.VMEM((2, 2, nz, 2) + block, BF16),
            pltpu.VMEM((chunks, 2, 2) + block, BF16),
            pltpu.VMEM((chunks, 2) + block, BF16),
            pltpu.VMEM((chunks, 2) + block, BF16),
            pltpu.VMEM((chunks,) + block, BF16),
            pltpu.VMEM((nz,) + block, BF16),
            pltpu.VMEM((nz,) + block, BF16),
            pltpu.VMEM((nz - 1,) + block, BF16),
            pltpu.VMEM((nz - 1,) + block, BF16),
            pltpu.VMEM(block, F32),
            pltpu.VMEM((chunks, tok, rows), BF16),
            pltpu.VMEM((tok, 1), F32),
            pltpu.VMEM((tok, 4 * cols), F32),
            pltpu.VMEM((chunks, 1, rows), F32),
            pltpu.VMEM((chunks, 1, rows), F32),
            pltpu.VMEM((7, 1, rows), F32),
            pltpu.VMEM((nz, 1, rows), F32),
            dma(4 * chunks - 1), dma(4 * chunks - 1),
            dma(chunks), dma(chunks), dma(chunks), dma(chunks),
            dma(nz), dma(nz), dma(nz - 1), dma(nz - 1), dma(7), dma(7),
            dma(nz - 1), dma(nz - 1), dma(7), dma(7),
        ],
        compiler_params=pltpu.CompilerParams(
            collective_id=0, has_side_effects=True, vmem_limit_bytes=56 * 2**20
        ),
    )(inputs, norm_gain.reshape(width // 128, 128), cotangent, weights)
    projected, gain_grad, new_weights, first, second = pl.pallas_call(
        finish,
        out_shape=(
            sd((tok, 4 * cols), BF16), sd((width // 128, 128), F32),
            sd(block, BF16), sd(block, BF16), sd(block, BF16),
        ),
        in_specs=[vm] * 6,
        out_specs=(vm,) * 5,
    )(projected, gains, grad, weights, first_moment, second_moment)
    return projected, gain_grad.reshape(width), new_weights.T, first.T, second.T


def solution(mesh):
    dp, node = mesh.shape["dp"], mesh.shape["node"]

    def body(inputs, norm_gain, cotangent, weights, first_moment, second_moment):
        args = (inputs, norm_gain, cotangent, weights, first_moment, second_moment)
        rows, cols = weights.shape
        if node == 4 and dp == 8 and rows % 128 == 0 and cols % 16 == 0:
            return per_device(dp // 2, *args)
        return plain(*args)

    return jax.shard_map(
        body,
        mesh=mesh,
        in_specs=(
            P(("dp", "node"), None),
            P(),
            P(("dp", "node"), None),
            P("dp", "node"),
            P("dp", "node"),
            P("dp", "node"),
        ),
        out_specs=(P(("dp", "node"), None), P(), P("dp", "node"), P("dp", "node"), P("dp", "node")),
        check_vma=False,
    )
```
